32 devices in a mesh: dp: 16 (over z, y, core), tensor: 2 (over x).
Axes of the slice: x: 2, y: 2, z: 4, core: 2. Of those that a mesh axis runs over, the one named last changes fastest.
Arguments:
- stream: bfloat16 [16, 1024, 1024], P('dp', 'tensor'), may hold values from -6 to 6
- norm_gain: float32 [1024], replicated, may hold values from 0.5 to 1.5
- proj_gate: bfloat16 [1024, 2048], P('dp', 'tensor'), may hold values from -0.1875 to 0.1875
- proj_input: bfloat16 [1024, 2048], P('dp', 'tensor'), may hold values from -0.1875 to 0.1875
- proj_state: bfloat16 [1024, 256], P('dp'), may hold values from -0.1875 to 0.1875
- proj_step: bfloat16 [1024, 32], P('dp', 'tensor'), may hold values from -0.1875 to 0.1875
- conv_input: float32 [4, 2048], P(None, 'tensor'), may hold values from -3 to 3
- conv_state: float32 [4, 256], replicated, may hold values from -3 to 3
- bias_input: float32 [2048], P('tensor'), may hold values from -0.5 to 0.5
- bias_state: float32 [256], replicated, may hold values from -0.5 to 0.5
- step_bias: float32 [32], P('tensor'), may hold values from -5 to -1
- decay_log: float32 [32], P('tensor'), may hold values from -3 to 1
- skip_gain: float32 [32], P('tensor'), may hold values from 0.5 to 1.5
- gate_gain: float32 [2048], P('tensor'), may hold values from 0.5 to 1.5
- proj_output: bfloat16 [2048, 1024], P('tensor', 'dp'), may hold values from -0.125 to 0.125
- cotangent: bfloat16 [16, 1024, 1024], P('dp', 'tensor'), may hold values from -6 to 6
Outputs:
- output: bfloat16 [16, 1024, 1024], P('dp', 'tensor')
- grad_stream: bfloat16 [16, 1024, 1024], P('dp', 'tensor')
- grad_norm_gain: float32 [1024], replicated
- grad_proj_gate: float32 [1024, 2048], P('dp', 'tensor')
- grad_proj_input: float32 [1024, 2048], P('dp', 'tensor')
- grad_proj_state: float32 [1024, 256], P('dp')
- grad_proj_step: float32 [1024, 32], P('dp', 'tensor')
- grad_conv_input: float32 [4, 2048], P(None, 'tensor')
- grad_conv_state: float32 [4, 256], replicated
- grad_bias_input: float32 [2048], P('tensor')
- grad_bias_state: float32 [256], replicated
- grad_step_bias: float32 [32], P('tensor')
- grad_decay_log: float32 [32], P('tensor')
- grad_skip_gain: float32 [32], P('tensor')
- grad_gate_gain: float32 [2048], P('tensor')
- grad_proj_output: float32 [2048, 1024], P('tensor', 'dp')
The draws below stay inside these ranges and needn't reach their ends.
All inputs are finite; a program needn't handle non-finite values.
Results may differ from the reference program's by a relative error of at most 0.017.
Values may be sent and summed in bfloat16 or wider, within the bound.
A program may use at most 192 MiB of HBM per device.

```python
import math
import jax
import jax.numpy as jnp
from jax import lax

D = 1024
H = 32
N = 128
KC = 4
SPAN = 256
LEN = 1024
DI = 2048
NSEQ = 16


def block_levels(rng, dims, shards, least, high):
    factor_of = 1.0
    for dim, parts in shards:
        heights = jax.random.uniform(jax.random.fold_in(jax.random.fold_in(rng, 6), dim), (parts,), jnp.float32, least / len(shards), high / len(shards))
        factor_of = factor_of * jnp.repeat(jnp.exp(heights), dims[dim] // parts).reshape((-1,) + (1,) * (len(dims) - 1 - dim))
    return factor_of


def centred(key, shape, spread, most, split=(), held_as=jnp.bfloat16):
    entries = jax.random.normal(key, shape, jnp.float32) * spread
    if len(split) > 0:
        entries = block_levels(key, shape, split, -0.22, 0.18) * entries
    return jnp.clip(entries, min=-most, max=most).astype(held_as)


def setup_inputs(seed: int = 0) -> dict:
    splits = jax.random.split(jax.random.key(seed), 17)
    stream = centred(splits[0], (NSEQ, LEN, D), 1.0, 6.0, ((0, 16), (1, 2)))
    norm_gain = jnp.clip(1.0 + 0.1 * jax.random.normal(splits[1], (D,), jnp.float32), 0.5, 1.5)
    proj_gate = centred(splits[2], (D, DI), D ** -0.5, 0.1875, ((0, 16), (1, 2)))
    proj_input = centred(splits[3], (D, DI), D ** -0.5, 0.1875, ((0, 16), (1, 2)))
    proj_state = centred(splits[4], (D, 2 * N), D ** -0.5, 0.1875, ((0, 16),))
    proj_step = centred(splits[5], (D, H), D ** -0.5, 0.1875, ((0, 16), (1, 2)))
    conv_input = centred(splits[6], (KC, DI), 0.5, 3.0, ((1, 2),), jnp.float32)
    conv_state = centred(splits[7], (KC, 2 * N), 0.5, 3.0, (), jnp.float32)
    bias_input = jnp.clip(jax.random.uniform(splits[8], (DI,), jnp.float32, -0.5, 0.5) * block_levels(splits[8], (DI,), ((0, 2),), -0.4, 0.0), -0.5, 0.5)
    bias_state = jnp.clip(jax.random.uniform(splits[9], (2 * N,), jnp.float32, -0.5, 0.5), -0.5, 0.5)
    step_bias = jnp.clip(-5.0 + 4.0 * jax.random.uniform(splits[10], (H,), jnp.float32) ** block_levels(splits[10], (H,), ((0, 2),), -0.2, 0.2), -5.0, -1.0)
    decay_log = jnp.clip(-3.0 + 4.0 * jax.random.uniform(splits[11], (H,), jnp.float32) ** block_levels(splits[11], (H,), ((0, 2),), -0.2, 0.2), -3.0, 1.0)
    skip_gain = jnp.clip(0.5 + 1.0 * jax.random.uniform(splits[12], (H,), jnp.float32) ** block_levels(splits[12], (H,), ((0, 2),), -0.2, 0.2), 0.5, 1.5)
    gate_gain = jnp.clip(1.0 + 0.1 * jax.random.normal(splits[13], (DI,), jnp.float32), 0.5, 1.5)
    proj_output = centred(splits[14], (DI, D), DI ** -0.5, 0.125, ((0, 2), (1, 16)))
    cotangent = centred(splits[15], (NSEQ, LEN, D), 1.0, 6.0, ((0, 16), (1, 2)))
    return {"stream": stream, "norm_gain": norm_gain, "proj_gate": proj_gate, "proj_input": proj_input, "proj_state": proj_state, "proj_step": proj_step, "conv_input": conv_input, "conv_state": conv_state, "bias_input": bias_input, "bias_state": bias_state, "step_bias": step_bias, "decay_log": decay_log, "skip_gain": skip_gain, "gate_gain": gate_gain, "proj_output": proj_output, "cotangent": cotangent}


EPS = 1e-05
HIGH_ACCURACY = lax.Precision.HIGHEST

@jax.custom_vjp
def low(v):
    return lax.optimization_barrier(v.astype(jnp.bfloat16)).astype(jnp.float32)

@jax.custom_vjp
def low_back(v):
    return v

def low_keep(v):
    return (low(v), None)

def low_pass(kept, grad):
    return (grad,)

def back_keep(v):
    return (v, None)

def back_low(kept, grad):
    return (low(grad),)
low.defvjp(low_keep, low_pass)
low_back.defvjp(back_keep, back_low)

def causal(values, kernel):
    tap_count = kernel.shape[0]
    length = values.shape[1]
    padded = jnp.pad(values, ((0, 0), (tap_count - 1, 0), (0, 0)))
    summed = kernel[0] * padded[:, 0:length]
    for tap_index in range(1, tap_count):
        summed = summed + kernel[tap_index] * padded[:, tap_index:tap_index + length]
    return summed

def span_scan(signal, dt_step, log_rate, b_rows, c_rows):
    seq_count, length, head_count, head_dim = signal.shape
    blocks = length // SPAN
    sig_blk = (signal * dt_step[..., None]).reshape(seq_count, blocks, SPAN, head_count, head_dim)
    rate_blk = jnp.moveaxis(log_rate.reshape(seq_count, blocks, SPAN, head_count), 3, 2)
    b_blk = b_rows.reshape(seq_count, blocks, SPAN, -1)
    c_blk = c_rows.reshape(seq_count, blocks, SPAN, -1)
    cumulative = jnp.cumsum(rate_blk, axis=-1)
    row_pos = lax.broadcasted_iota(jnp.int32, (SPAN, SPAN), 0)
    col_pos = lax.broadcasted_iota(jnp.int32, (SPAN, SPAN), 1)
    gap_sum = cumulative[..., :, None] - cumulative[..., None, :]
    weights = jnp.exp(jnp.where(row_pos >= col_pos, gap_sum, -jnp.inf))
    scores = jnp.einsum('scqn,scrn->scqr', c_blk, b_blk, precision=HIGH_ACCURACY)
    blended = scores[:, :, None] * weights
    y_within = jnp.einsum('schqr,scrhp->scqhp', blended, sig_blk, precision=HIGH_ACCURACY)
    to_end = jnp.exp(cumulative[..., -1:] - cumulative)
    states = jnp.einsum('scrn,schr,scrhp->schnp', b_blk, to_end, sig_blk, precision=HIGH_ACCURACY)
    carried = jnp.exp(cumulative[..., -1])

    def advance(previous, inputs):
        span_state, factor = inputs
        return (factor[..., None, None] * previous + span_state, previous)
    initial = jnp.zeros(states.shape[:1] + states.shape[2:], states.dtype)
    _, entering = lax.scan(advance, initial, (jnp.moveaxis(states, 1, 0), jnp.moveaxis(carried, 1, 0)))
    entering = jnp.moveaxis(entering, 0, 1)
    y_across = jnp.einsum('scqn,schq,schnp->scqhp', c_blk, jnp.exp(cumulative), entering, precision=HIGH_ACCURACY)
    return (y_within + y_across).reshape(seq_count, length, head_count, head_dim)

def mixer(gate_pre, input_pre, state_pre, step_pre, conv_input, conv_state, bias_input, bias_state, step_bias, decay_log, skip_gain):
    seq_count, length, channels = input_pre.shape
    head_count = step_pre.shape[-1]
    signal = jax.nn.silu(causal(input_pre, conv_input) + bias_input)
    state_in = jax.nn.silu(causal(state_pre, conv_state) + bias_state)
    half_width = state_in.shape[-1] // 2
    dt_step = jax.nn.softplus(step_pre + step_bias)
    log_rate = -jnp.exp(decay_log) * dt_step
    heads_sig = signal.reshape(seq_count, length, head_count, channels // head_count)
    scanned = span_scan(heads_sig, dt_step, log_rate, state_in[..., :half_width], state_in[..., half_width:])
    scanned = scanned + skip_gain[:, None] * heads_sig
    return scanned.reshape(seq_count, length, channels) * jax.nn.silu(gate_pre)

def reference(stream, norm_gain, proj_gate, proj_input, proj_state, proj_step, conv_input, conv_state, bias_input, bias_state, step_bias, decay_log, skip_gain, gate_gain, proj_output, cotangent):
    group_size = math.gcd(NSEQ, max(1, 4096 // LEN))
    params = (norm_gain, proj_gate.astype(jnp.float32), proj_input.astype(jnp.float32), proj_state.astype(jnp.float32), proj_step.astype(jnp.float32), conv_input, conv_state, bias_input, bias_state, step_bias, decay_log, skip_gain, gate_gain, proj_output.astype(jnp.float32))

    def forward(stream_f, n_gain, p_gate, p_input, p_state, p_step, c_input, c_state, b_input, b_state, s_bias, d_log, s_gain, g_gain, p_output):

        def one_group(rows_f):
            inv_rms = lax.rsqrt(lax.optimization_barrier(jnp.mean(rows_f * rows_f, axis=-1, keepdims=True)) + EPS)
            hidden_values = low(rows_f * inv_rms * n_gain)

            def project(weight_matrix):
                return low_back(jnp.einsum('nbp,pr->nbr', hidden_values, weight_matrix, precision=HIGH_ACCURACY))
            mixed = mixer(project(p_gate), project(p_input), project(p_state), project(p_step), c_input, c_state, b_input, b_state, s_bias, d_log, s_gain)
            scale = lax.rsqrt(lax.optimization_barrier(jnp.mean(mixed * mixed, axis=-1, keepdims=True)) + EPS)
            gated = low(mixed * scale * g_gain)
            return rows_f + jnp.einsum('slc,ce->sle', gated, p_output, precision=HIGH_ACCURACY)
        grouped = stream_f.reshape(NSEQ // group_size, group_size, LEN, D)
        result = lax.map(jax.checkpoint(one_group), grouped)
        return result.reshape(NSEQ, LEN, D)
    result, pull = jax.vjp(forward, stream.astype(jnp.float32), *params)
    grads = pull(cotangent.astype(jnp.float32))
    return (result.astype(jnp.bfloat16), grads[0].astype(jnp.bfloat16), grads[1], grads[2], grads[3], grads[4], grads[5], grads[6], grads[7], grads[8], grads[9], grads[10], grads[11], grads[12], grads[13], grads[14])
```

```python
import jax
import jax.numpy as jnp
from jax import lax
from jax.experimental import pallas as pl
from jax.experimental.pallas import tpu as pltpu
from jax.sharding import PartitionSpec as P

SPAN = 256
DI = 2048
HEAD = 64
STATE = 128
EPS = 1e-05
F32 = jnp.float32
BF16 = jnp.bfloat16
VMEM_LIMIT = 48 * 1024 * 1024


def dot(a, b, ca, cb):
    return lax.dot_general(a, b, (((ca,), (cb,)), ((), ())), preferred_element_type=F32)


def sigmoid(v):
    return 1.0 / (1.0 + jnp.exp(-v))


def later(v, s):
    if s == 0:
        return v
    lane = lax.broadcasted_iota(jnp.int32, v.shape, 1)
    return jnp.where(lane >= s, pltpu.roll(v, s, 1), 0.0)


def earlier(v, s):
    if s == 0:
        return v
    length = v.shape[1]
    lane = lax.broadcasted_iota(jnp.int32, v.shape, 1)
    return jnp.where(lane < length - s, pltpu.roll(v, length - s, 1), 0.0)


def conv(x, par):
    v = par[:, 4:5] + par[:, 3:4] * x
    for k in range(3):
        v = v + par[:, k : k + 1] * later(x, 3 - k)
    return v


def conv_back(dv, par):
    g = par[:, 3:4] * dv
    for k in range(3):
        g = g + par[:, k : k + 1] * earlier(dv, 3 - k)
    return g


def total(v):
    return jnp.sum(v, axis=1, keepdims=True)


def columns(cols):
    lane = lax.broadcasted_iota(jnp.int32, (cols[0].shape[0], 128), 1)
    out = jnp.zeros(lane.shape, F32)
    for i, c in enumerate(cols):
        out = jnp.where(lane == i, c, out)
    return out


def decay(cq):
    q = cq.shape[1]
    col = jnp.broadcast_to(cq, (128, q)).T
    col = jnp.concatenate([col] * (q // 128), axis=1)
    r_pos = lax.broadcasted_iota(jnp.int32, (q, q), 0)
    q_pos = lax.broadcasted_iota(jnp.int32, (q, q), 1)
    return jnp.exp(jnp.where(q_pos >= r_pos, cq - col, -jnp.inf))


def fwd_kernel(xpre, gate, spre, rows, par, spar, y_out, mixed_out, sq_out, s_out, bc_out, scores):
    h = pl.program_id(0)
    blocks = scores.shape[0]

    @pl.when(h == 0)
    def _():
        v = conv(spre[...], spar[...])
        bc_out[...] = (v * sigmoid(v)).astype(BF16)
        sq_out[...] = jnp.zeros_like(sq_out)
        for c in range(blocks):
            sl = slice(c * SPAN, (c + 1) * SPAN)
            scores[c] = dot(bc_out[:STATE, sl], bc_out[STATE:, sl], 0, 0)

    v = conv(xpre[...], par[...])
    x = v * sigmoid(v)
    cum = rows[0:1, :]
    u = x * rows[1:2, :]
    ub = u.astype(BF16)
    state = jnp.zeros((HEAD, STATE), F32)
    for c in range(blocks):
        sl = slice(c * SPAN, (c + 1) * SPAN)
        cq = cum[:, sl]
        last = cq[:, SPAN - 1 :]
        pt = (scores[c] * decay(cq)).astype(BF16)
        sb = state.astype(BF16)
        s_out[c] = state
        y_out[:, sl] = dot(ub[:, sl], pt, 1, 0) + jnp.exp(cq) * dot(sb, bc_out[STATE:, sl], 1, 0)
        ute = (u[:, sl] * jnp.exp(last - cq)).astype(BF16)
        state = jnp.exp(last) * state + dot(ute, bc_out[:STATE, sl], 1, 1)
    g = gate[...]
    mixed = (y_out[...] + par[:, 5:6] * x) * (g * sigmoid(g))
    mixed_out[...] = mixed
    sq_out[...] += jnp.sum(mixed * mixed, axis=0, keepdims=True)


def bwd_kernel(
    xpre, gate, y_in, gg_in, s_in, rows, tok, bc, par,
    gx_out, ggate_out, cols_out, rows_out, dbc_out, scores, dscores, dbc,
):
    h = pl.program_id(0)
    blocks = scores.shape[0]

    @pl.when(h == 0)
    def _():
        for c in range(blocks):
            sl = slice(c * SPAN, (c + 1) * SPAN)
            scores[c] = dot(bc[:STATE, sl], bc[STATE:, sl], 0, 0)
        dscores[...] = jnp.zeros_like(dscores)
        dbc[...] = jnp.zeros_like(dbc)

    x0 = xpre[...]
    v = conv(x0, par[...])
    sg = sigmoid(v)
    x = v * sg
    skip = par[:, 5:6]
    cum = rows[0:1, :]
    dt = rows[1:2, :]
    scale = tok[0:1, :]
    g = gate[...]
    sgate = sigmoid(g)
    silu_g = g * sgate
    y = y_in[...]
    gg = gg_in[...]
    scanned = y + skip * x
    mixed = scanned * silu_g
    gm = scale * gg * par[:, 6:7] - mixed * tok[1:2, :]
    ggate_out[...] = (gm * scanned * (sgate * (1.0 + g * (1.0 - sgate)))).astype(BF16)
    dgain = total(gg * mixed * scale)
    dy = gm * silu_g
    dskip = total(dy * x)
    dyb = dy.astype(BF16)
    dyf = dyb.astype(F32)
    out_dot = jnp.sum(dyf * y, axis=0, keepdims=True)
    u = x * dt
    ub = u.astype(BF16)
    uf = ub.astype(F32)
    lane = lax.broadcasted_iota(jnp.int32, (1, SPAN), 1)
    grad = jnp.zeros((HEAD, STATE), F32)
    du_parts = []
    dcum_parts = []
    for c in reversed(range(blocks)):
        sl = slice(c * SPAN, (c + 1) * SPAN)
        cq = cum[:, sl]
        last = cq[:, SPAN - 1 :]
        te = jnp.exp(last - cq)
        ec = jnp.exp(cq)
        b_c = bc[:STATE, sl]
        c_c = bc[STATE:, sl]
        w = decay(cq)
        pt = (scores[c] * w).astype(BF16)
        dpt = dot(ub[:, sl], dyb[:, sl], 0, 0)
        dscores[c] += dpt * w
        gb = grad.astype(BF16)
        state = s_in[c]
        du1 = dot(dyb[:, sl], pt, 1, 1)
        du2 = dot(gb, b_c, 1, 0) * te
        du = du1 + du2
        through = uf[:, sl] * du2
        at_end = jnp.sum(through) + jnp.sum(jnp.exp(last) * grad * state)
        dc = out_dot[:, sl] - jnp.sum(uf[:, sl] * du1 + through, axis=0, keepdims=True)
        dcum_parts.append(dc + jnp.where(lane == SPAN - 1, at_end, 0.0))
        du_parts.append(du)
        edy = (dyf[:, sl] * ec).astype(BF16)
        dbc[STATE:, sl] += dot(state.astype(BF16), edy, 0, 0)
        dbc[:STATE, sl] += dot(gb, (u[:, sl] * te).astype(BF16), 0, 0)
        grad = jnp.exp(last) * grad + dot(edy, c_c, 1, 1)
    du = jnp.concatenate(du_parts[::-1], axis=1)
    rows_out[0:1, :] = jnp.concatenate(dcum_parts[::-1], axis=1)
    rows_out[1:2, :] = jnp.sum(x * du, axis=0, keepdims=True)
    dv = (du * dt + skip * dy) * (sg * (1.0 + v * (1.0 - sg)))
    gx_out[...] = conv_back(dv, par[...]).astype(BF16)
    cols = [total(dv * later(x0, 3 - k)) for k in range(4)]
    cols_out[...] = columns(cols + [total(dv), dskip, dgain])

    @pl.when(h == pl.num_programs(0) - 1)
    def _():
        for c in range(blocks):
            sl = slice(c * SPAN, (c + 1) * SPAN)
            ds = dscores[c].astype(BF16)
            dbc_out[:STATE, sl] = (dbc[:STATE, sl] + dot(bc[STATE:, sl], ds, 1, 1)).astype(BF16)
            dbc_out[STATE:, sl] = (dbc[STATE:, sl] + dot(bc[:STATE, sl], ds, 1, 0)).astype(BF16)


def state_kernel(spre, dbc, spar, g_out, cols_out):
    x0 = spre[...]
    v = conv(x0, spar[...])
    sg = sigmoid(v)
    dv = dbc[...].astype(F32) * (sg * (1.0 + v * (1.0 - sg)))
    g_out[...] = conv_back(dv, spar[...]).astype(BF16)
    cols = [total(dv * later(x0, 3 - k)) for k in range(4)]
    cols_out[...] = columns(cols + [total(dv)])


def cost(flops, size):
    return pl.CostEstimate(flops=flops, bytes_accessed=size, transcendentals=0)


PARAMS = pltpu.CompilerParams(
    dimension_semantics=("arbitrary",), vmem_limit_bytes=VMEM_LIMIT
)


def specs(length):
    chan = pl.BlockSpec((HEAD, length), lambda h: (h, 0))
    rows = pl.BlockSpec((None, 2, length), lambda h: (h, 0, 0))
    par = pl.BlockSpec((HEAD, 8), lambda h: (h, 0))
    states = pl.BlockSpec((None, length // SPAN, HEAD, STATE), lambda h: (h, 0, 0, 0))
    whole = lambda *shape: pl.BlockSpec(shape, lambda h: (0,) * len(shape))
    return chan, rows, par, states, whole


def scan_fwd(xpre, gate, spre, rows, par, spar):
    inner, length = xpre.shape
    heads, blocks = inner // HEAD, length // SPAN
    chan, row, parb, states, whole = specs(length)
    sds = jax.ShapeDtypeStruct
    return pl.pallas_call(
        fwd_kernel,
        grid=(heads,),
        in_specs=[chan, chan, whole(2 * STATE, length), row, parb, whole(2 * STATE, 8)],
        out_specs=[chan, chan, whole(1, length), states, whole(2 * STATE, length)],
        out_shape=[
            sds((inner, length), F32),
            sds((inner, length), F32),
            sds((1, length), F32),
            sds((heads, blocks, HEAD, STATE), F32),
            sds((2 * STATE, length), BF16),
        ],
        scratch_shapes=[pltpu.VMEM((blocks, SPAN, SPAN), F32)],
        compiler_params=PARAMS,
        cost_estimate=cost(12 * 10**9, 20 * 10**6),
    )(xpre, gate, spre, rows, par, spar)


def scan_bwd(xpre, gate, y, gg, states_in, rows, tok, bc, par):
    inner, length = xpre.shape
    heads, blocks = inner // HEAD, length // SPAN
    chan, row, parb, states, whole = specs(length)
    sds = jax.ShapeDtypeStruct
    return pl.pallas_call(
        bwd_kernel,
        grid=(heads,),
        in_specs=[
            chan, chan, chan, chan, states, row,
            whole(2, length), whole(2 * STATE, length), parb,
        ],
        out_specs=[
            chan, chan, pl.BlockSpec((HEAD, 128), lambda h: (h, 0)), row,
            whole(2 * STATE, length),
        ],
        out_shape=[
            sds((inner, length), BF16),
            sds((inner, length), BF16),
            sds((inner, 128), F32),
            sds((heads, 2, length), F32),
            sds((2 * STATE, length), BF16),
        ],
        scratch_shapes=[
            pltpu.VMEM((blocks, SPAN, SPAN), F32),
            pltpu.VMEM((blocks, SPAN, SPAN), F32),
            pltpu.VMEM((2 * STATE, length), F32),
        ],
        compiler_params=PARAMS,
        cost_estimate=cost(30 * 10**9, 30 * 10**6),
    )(xpre, gate, y, gg, states_in, rows, tok, bc, par)


def state_bwd(spre, dbc, spar):
    sds = jax.ShapeDtypeStruct
    return pl.pallas_call(
        state_kernel,
        out_shape=[sds(spre.shape, BF16), sds((spre.shape[0], 128), F32)],
        compiler_params=pltpu.CompilerParams(vmem_limit_bytes=VMEM_LIMIT),
        cost_estimate=cost(10**9, 2 * 10**6),
    )(spre, dbc, spar)


def bits_of(n):
    return n.bit_length() - 1


def swap(v, axis, n, bit):
    return lax.ppermute(v, axis, [(i, i ^ (1 << bit)) for i in range(n)])


def sum_all(v, axis, n):
    for bit in range(bits_of(n)):
        v = v + swap(v, axis, n, bit)
    return v


def sum_scatter(v, axis, n, order, last=F32):
    me = lax.axis_index(axis)
    rows, rest = v.shape[0] // n, v.shape[1:]
    left = list(range(bits_of(n)))[::-1]
    v = v.reshape((2,) * len(left) + (rows,) + rest)
    for i, bit in enumerate(order):
        dim = left.index(bit)
        mine = (me >> bit) & 1
        keep = lax.dynamic_index_in_dim(v, mine, dim, keepdims=False)
        send = lax.dynamic_index_in_dim(v, 1 - mine, dim, keepdims=False)
        left.remove(bit)
        got = swap(send, axis, n, bit)
        v = keep.astype(F32) + got.astype(F32)
        if i < len(order) - 1:
            v = v.astype(BF16)
    return v.astype(last)


def local(
    dp_size,
    tp_size,
    stream,
    norm_gain,
    proj_gate,
    proj_input,
    proj_state,
    proj_step,
    conv_input,
    conv_state,
    bias_input,
    bias_state,
    step_bias,
    decay_log,
    skip_gain,
    gate_gain,
    proj_output,
    cotangent,
):
    inner = conv_input.shape[1]
    heads = inner // HEAD
    own_rows = stream.shape[1]
    length = own_rows * tp_size
    blocks = length // SPAN
    dp_order = [0, 1] + list(range(bits_of(dp_size)))[2:][::-1]
    tp_order = list(range(bits_of(tp_size)))[::-1]
    stream_f = stream[0].astype(F32)
    inv_rms = lax.rsqrt(jnp.mean(stream_f * stream_f, axis=-1, keepdims=True) + EPS)
    normed = stream_f * inv_rms
    own_hidden = (normed * norm_gain).astype(BF16)
    hidden = lax.all_gather(own_hidden, "tensor", axis=0, tiled=True)
    cot = lax.all_gather(cotangent[0], "tensor", axis=0, tiled=True)
    input_w = lax.all_gather(proj_input, "dp", axis=0, tiled=True)
    small_w = lax.all_gather(
        jnp.concatenate([proj_state, proj_step], axis=1), "dp", axis=0, tiled=True
    )
    gate_w = lax.all_gather(proj_gate, "dp", axis=0, tiled=True)
    out_w = lax.all_gather(proj_output.T, "dp", axis=0, tiled=True)
    n_state = proj_state.shape[1]

    def project(w):
        return jnp.einsum("lp,pr->rl", hidden, w, preferred_element_type=F32)

    input_pre = project(input_w)
    small_pre = project(small_w)
    state_pre, step_pre = small_pre[:n_state], small_pre[n_state:]
    gate_pre = project(gate_w)

    step_in = step_pre + step_bias[:, None]
    dt = jax.nn.softplus(step_in)
    neg = -jnp.exp(decay_log)[:, None]
    rate = neg * dt
    tri = jnp.triu(jnp.ones((SPAN, SPAN), F32))
    cum = jnp.einsum(
        "hbt,tq->hbq", rate.reshape(heads, blocks, SPAN), tri, precision=lax.Precision.HIGHEST
    ).reshape(heads, length)
    rows = jnp.stack([cum, dt], axis=1)
    zero = jnp.zeros((inner, 1), F32)
    par = jnp.concatenate(
        [
            conv_input.T,
            bias_input[:, None],
            jnp.repeat(skip_gain, HEAD)[:, None],
            gate_gain[:, None],
            zero,
        ],
        axis=1,
    )
    spar = jnp.concatenate(
        [conv_state.T, bias_state[:, None], jnp.zeros((n_state, 3), F32)], axis=1
    )
    y, mixed, square, states, bc = scan_fwd(input_pre, gate_pre, state_pre, rows, par, spar)

    grad_gated = jnp.einsum("le,ec->cl", cot, out_w, preferred_element_type=F32)
    inner_dot = jnp.sum(grad_gated * gate_gain[:, None] * mixed, axis=0, keepdims=True)
    sums = sum_all(jnp.concatenate([square, inner_dot], axis=0), "tensor", tp_size)
    scale = lax.rsqrt(sums[0:1] / DI + EPS)
    tok = jnp.concatenate([scale, scale * scale * scale * (sums[1:2] / DI)], axis=0)
    gated = (mixed * scale * gate_gain[:, None]).astype(BF16)
    grad_out_w = jnp.einsum("cl,le->ec", gated, cot, preferred_element_type=F32).astype(BF16)
    shard_out = sum_scatter(grad_out_w, "dp", dp_size, dp_order)
    partial_out = jnp.einsum("cl,ec->le", gated, out_w, preferred_element_type=F32).astype(BF16)
    branch = sum_scatter(partial_out, "tensor", tp_size, tp_order)
    output = (stream_f + branch).astype(BF16)

    gx, ggate, cols, drows, dbc = scan_bwd(
        input_pre, gate_pre, y, grad_gated, states, rows, tok, bc, par
    )
    dbc_total = sum_all(dbc.astype(BF16), "tensor", tp_size)
    gstate, scols = state_bwd(state_pre, dbc_total, spar)
    drate = jnp.einsum(
        "hbt,qt->hbq",
        drows[:, 0].reshape(heads, blocks, SPAN),
        tri,
        precision=lax.Precision.HIGHEST,
    ).reshape(heads, length)
    ddt = drows[:, 1] + drate * neg
    ddecay = jnp.sum(drate * rate, axis=1)
    dstep = ddt * jax.nn.sigmoid(step_in)
    dstep_bias = jnp.sum(dstep, axis=1)
    gstep = dstep.astype(BF16)

    def weight_grad(g):
        return jnp.einsum("lk,cl->kc", hidden, g, preferred_element_type=F32).astype(BF16)

    shard_input = sum_scatter(weight_grad(gx), "dp", dp_size, dp_order)
    shard_gate = sum_scatter(weight_grad(ggate), "dp", dp_size, dp_order)
    shard_small = sum_scatter(
        weight_grad(jnp.concatenate([gstate, gstep], axis=0)), "dp", dp_size, dp_order
    )

    def back(g, w):
        return jnp.einsum("cl,nc->ln", g, w, preferred_element_type=F32)

    state_w, step_w = small_w[:, :n_state], small_w[:, n_state:]
    back_terms = back(ggate, gate_w) + back(gx, input_w) + back(gstep, step_w)
    grad_hidden = sum_scatter(back_terms.astype(BF16), "tensor", tp_size, tp_order)
    row_start = lax.axis_index("tensor") * own_rows
    own_gstate = lax.dynamic_slice_in_dim(gstate, row_start, own_rows, 1)
    grad_hidden = grad_hidden + back(own_gstate, state_w)
    weighted_h = grad_hidden * norm_gain
    norm_dot = jnp.mean(weighted_h * normed, axis=-1, keepdims=True)
    grad_stream = (
        cotangent[0].astype(F32) + inv_rms * (weighted_h - normed * norm_dot)
    ).astype(BF16)
    norm_part = sum_all(jnp.sum(grad_hidden * normed, axis=0), "tensor", tp_size)

    pieces = [
        cols[:, :4].T,
        cols[:, 4],
        jnp.sum(cols[:, 5].reshape(heads, HEAD), axis=1),
        cols[:, 6],
        scols[:, :4].T,
        scols[:, 4],
        dstep_bias,
        ddecay,
        norm_part,
    ]
    flat = jnp.concatenate([p.reshape(-1) for p in pieces])
    pad = -flat.shape[0] % 1024
    flat = jnp.pad(flat, (0, pad)).reshape(-1, 128)
    flat = sum_all(flat, "dp", dp_size).reshape(-1)
    done, at = [], 0
    for p in pieces:
        done.append(flat[at : at + p.size].reshape(p.shape))
        at += p.size
    conv_in_g, bias_in_g, skip_g, gain_g, conv_st_g, bias_st_g, step_b_g, decay_g, norm_g = done
    return (
        output[None],
        grad_stream[None],
        norm_g,
        shard_gate,
        shard_input,
        shard_small[:, :n_state],
        shard_small[:, n_state:],
        conv_in_g,
        conv_st_g,
        bias_in_g,
        bias_st_g,
        step_b_g,
        decay_g,
        skip_g,
        gain_g,
        shard_out.T,
    )


def solution(mesh):
    placed = (
        P("dp", "tensor", None),
        P(),
        P("dp", "tensor"),
        P("dp", "tensor"),
        P("dp", None),
        P("dp", "tensor"),
        P(None, "tensor"),
        P(),
        P("tensor"),
        P(),
        P("tensor"),
        P("tensor"),
        P("tensor"),
        P("tensor"),
        P("tensor", "dp"),
        P("dp", "tensor", None),
    )
    dp_size, tp_size = mesh.shape["dp"], mesh.shape["tensor"]

    def run(*args):
        return local(dp_size, tp_size, *args)

    return jax.shard_map(
        run,
        mesh=mesh,
        in_specs=placed,
        out_specs=(
            P("dp", "tensor", None),
            P("dp", "tensor", None),
            P(),
            P("dp", "tensor"),
            P("dp", "tensor"),
            P("dp", None),
            P("dp", "tensor"),
            P(None, "tensor"),
            P(),
            P("tensor"),
            P(),
            P("tensor"),
            P("tensor"),
            P("tensor"),
            P("tensor"),
            P("tensor", "dp"),
        ),
        check_vma=False,
    )
```

```python
import jax
import jax.numpy as jnp
from jax import lax
from jax.experimental import pallas as pl
from jax.experimental.pallas import tpu as pltpu
from jax.sharding import PartitionSpec as P

SPAN = 256
DI = 2048
HEAD = 64
STATE = 128
EPS = 1e-05
F32 = jnp.float32
BF16 = jnp.bfloat16
VMEM_LIMIT = 48 * 1024 * 1024


def dot(a, b, ca, cb):
    return lax.dot_general(a, b, (((ca,), (cb,)), ((), ())), preferred_element_type=F32)


def sigmoid(v):
    return 1.0 / (1.0 + jnp.exp(-v))


def later(v, s):
    if s == 0:
        return v
    lane = lax.broadcasted_iota(jnp.int32, v.shape, 1)
    return jnp.where(lane >= s, pltpu.roll(v, s, 1), 0.0)


def earlier(v, s):
    if s == 0:
        return v
    length = v.shape[1]
    lane = lax.broadcasted_iota(jnp.int32, v.shape, 1)
    return jnp.where(lane < length - s, pltpu.roll(v, length - s, 1), 0.0)


def conv(x, par):
    v = par[:, 4:5] + par[:, 3:4] * x
    for k in range(3):
        v = v + par[:, k : k + 1] * later(x, 3 - k)
    return v


def conv_back(dv, par):
    g = par[:, 3:4] * dv
    for k in range(3):
        g = g + par[:, k : k + 1] * earlier(dv, 3 - k)
    return g


def total(v):
    return jnp.sum(v, axis=1, keepdims=True)


def columns(cols):
    lane = lax.broadcasted_iota(jnp.int32, (cols[0].shape[0], 128), 1)
    out = jnp.zeros(lane.shape, F32)
    for i, c in enumerate(cols):
        out = jnp.where(lane == i, c, out)
    return out


def decay(cq):
    q = cq.shape[1]
    col = jnp.broadcast_to(cq, (128, q)).T
    col = jnp.concatenate([col] * (q // 128), axis=1)
    r_pos = lax.broadcasted_iota(jnp.int32, (q, q), 0)
    q_pos = lax.broadcasted_iota(jnp.int32, (q, q), 1)
    return jnp.exp(jnp.where(q_pos >= r_pos, cq - col, -jnp.inf))


def fwd_kernel(xpre, gate, spre, rows, par, spar, y_out, mixed_out, sq_out, s_out, bc_out, scores):
    h = pl.program_id(0)
    blocks = scores.shape[0]

    @pl.when(h == 0)
    def _():
        v = conv(spre[...], spar[...])
        bc_out[...] = (v * sigmoid(v)).astype(BF16)
        sq_out[...] = jnp.zeros_like(sq_out)
        for c in range(blocks):
            sl = slice(c * SPAN, (c + 1) * SPAN)
            scores[c] = dot(bc_out[:STATE, sl], bc_out[STATE:, sl], 0, 0)

    v = conv(xpre[...], par[...])
    x = v * sigmoid(v)
    cum = rows[0:1, :]
    u = x * rows[1:2, :]
    ub = u.astype(BF16)
    state = jnp.zeros((HEAD, STATE), F32)
    for c in range(blocks):
        sl = slice(c * SPAN, (c + 1) * SPAN)
        cq = cum[:, sl]
        last = cq[:, SPAN - 1 :]
        pt = (scores[c] * decay(cq)).astype(BF16)
        sb = state.astype(BF16)
        s_out[c] = state
        y_out[:, sl] = dot(ub[:, sl], pt, 1, 0) + jnp.exp(cq) * dot(sb, bc_out[STATE:, sl], 1, 0)
        ute = (u[:, sl] * jnp.exp(last - cq)).astype(BF16)
        state = jnp.exp(last) * state + dot(ute, bc_out[:STATE, sl], 1, 1)
    g = gate[...]
    mixed = (y_out[...] + par[:, 5:6] * x) * (g * sigmoid(g))
    mixed_out[...] = mixed
    sq_out[...] += jnp.sum(mixed * mixed, axis=0, keepdims=True)


def bwd_kernel(
    xpre, gate, y_in, gg_in, s_in, rows, tok, bc, par,
    gx_out, ggate_out, cols_out, rows_out, dbc_out, scores, dscores, dbc,
):
    h = pl.program_id(0)
    blocks = scores.shape[0]

    @pl.when(h == 0)
    def _():
        for c in range(blocks):
            sl = slice(c * SPAN, (c + 1) * SPAN)
            scores[c] = dot(bc[:STATE, sl], bc[STATE:, sl], 0, 0)
        dscores[...] = jnp.zeros_like(dscores)
        dbc[...] = jnp.zeros_like(dbc)

    x0 = xpre[...]
    v = conv(x0, par[...])
    sg = sigmoid(v)
    x = v * sg
    skip = par[:, 5:6]
    cum = rows[0:1, :]
    dt = rows[1:2, :]
    scale = tok[0:1, :]
    g = gate[...]
    sgate = sigmoid(g)
    silu_g = g * sgate
    y = y_in[...]
    gg = gg_in[...]
    scanned = y + skip * x
    mixed = scanned * silu_g
    gm = scale * gg * par[:, 6:7] - mixed * tok[1:2, :]
    ggate_out[...] = (gm * scanned * (sgate * (1.0 + g * (1.0 - sgate)))).astype(BF16)
    dgain = total(gg * mixed * scale)
    dy = gm * silu_g
    dskip = total(dy * x)
    dyb = dy.astype(BF16)
    dyf = dyb.astype(F32)
    out_dot = jnp.sum(dyf * y, axis=0, keepdims=True)
    u = x * dt
    ub = u.astype(BF16)
    uf = ub.astype(F32)
    lane = lax.broadcasted_iota(jnp.int32, (1, SPAN), 1)
    grad = jnp.zeros((HEAD, STATE), F32)
    du_parts = []
    dcum_parts = []
    for c in reversed(range(blocks)):
        sl = slice(c * SPAN, (c + 1) * SPAN)
        cq = cum[:, sl]
        last = cq[:, SPAN - 1 :]
        te = jnp.exp(last - cq)
        ec = jnp.exp(cq)
        b_c = bc[:STATE, sl]
        c_c = bc[STATE:, sl]
        w = decay(cq)
        pt = (scores[c] * w).astype(BF16)
        dpt = dot(ub[:, sl], dyb[:, sl], 0, 0)
        dscores[c] += dpt * w
        gb = grad.astype(BF16)
        state = s_in[c]
        du1 = dot(dyb[:, sl], pt, 1, 1)
        du2 = dot(gb, b_c, 1, 0) * te
        du = du1 + du2
        through = uf[:, sl] * du2
        at_end = jnp.sum(through) + jnp.sum(jnp.exp(last) * grad * state)
        dc = out_dot[:, sl] - jnp.sum(uf[:, sl] * du1 + through, axis=0, keepdims=True)
        dcum_parts.append(dc + jnp.where(lane == SPAN - 1, at_end, 0.0))
        du_parts.append(du)
        edy = (dyf[:, sl] * ec).astype(BF16)
        dbc[STATE:, sl] += dot(state.astype(BF16), edy, 0, 0)
        dbc[:STATE, sl] += dot(gb, (u[:, sl] * te).astype(BF16), 0, 0)
        grad = jnp.exp(last) * grad + dot(edy, c_c, 1, 1)
    du = jnp.concatenate(du_parts[::-1], axis=1)
    rows_out[0:1, :] = jnp.concatenate(dcum_parts[::-1], axis=1)
    rows_out[1:2, :] = jnp.sum(x * du, axis=0, keepdims=True)
    dv = (du * dt + skip * dy) * (sg * (1.0 + v * (1.0 - sg)))
    gx_out[...] = conv_back(dv, par[...]).astype(BF16)
    cols = [total(dv * later(x0, 3 - k)) for k in range(4)]
    cols_out[...] = columns(cols + [total(dv), dskip, dgain])

    @pl.when(h == pl.num_programs(0) - 1)
    def _():
        for c in range(blocks):
            sl = slice(c * SPAN, (c + 1) * SPAN)
            ds = dscores[c].astype(BF16)
            dbc_out[:STATE, sl] = (dbc[:STATE, sl] + dot(bc[STATE:, sl], ds, 1, 1))
            dbc_out[STATE:, sl] = (dbc[STATE:, sl] + dot(bc[:STATE, sl], ds, 1, 0))


def state_kernel(spre, dbc, spar, g_out, cols_out):
    x0 = spre[...]
    v = conv(x0, spar[...])
    sg = sigmoid(v)
    dv = dbc[...].astype(F32) * (sg * (1.0 + v * (1.0 - sg)))
    g_out[...] = conv_back(dv, spar[...]).astype(BF16)
    cols = [total(dv * later(x0, 3 - k)) for k in range(4)]
    cols_out[...] = columns(cols + [total(dv)])


def cost(flops, size):
    return pl.CostEstimate(flops=flops, bytes_accessed=size, transcendentals=0)


PARAMS = pltpu.CompilerParams(
    dimension_semantics=("arbitrary",), vmem_limit_bytes=VMEM_LIMIT
)


def specs(length, first=0):
    chan = pl.BlockSpec((HEAD, length), lambda h: (h + first, 0))
    rows = pl.BlockSpec((None, 2, length), lambda h: (h + first, 0, 0))
    par = pl.BlockSpec((HEAD, 8), lambda h: (h + first, 0))
    states = pl.BlockSpec(
        (None, length // SPAN, HEAD, STATE), lambda h: (h + first, 0, 0, 0)
    )
    whole = lambda *shape: pl.BlockSpec(shape, lambda h: (0,) * len(shape))
    return chan, rows, par, states, whole


def scan_fwd(pre, gate, rows, par, spar):
    inner, length = gate.shape
    heads, blocks = inner // HEAD, length // SPAN
    chan, row, parb, states, whole = specs(length)
    sds = jax.ShapeDtypeStruct
    return pl.pallas_call(
        fwd_kernel,
        grid=(heads,),
        in_specs=[
            chan, chan,
            pl.BlockSpec((2 * STATE, length), lambda h: (inner // (2 * STATE), 0)),
            row, parb, whole(2 * STATE, 8),
        ],
        out_specs=[chan, chan, whole(1, length), states, whole(2 * STATE, length)],
        out_shape=[
            sds((inner, length), F32),
            sds((inner, length), F32),
            sds((1, length), F32),
            sds((heads, blocks, HEAD, STATE), F32),
            sds((2 * STATE, length), BF16),
        ],
        scratch_shapes=[pltpu.VMEM((blocks, SPAN, SPAN), F32)],
        compiler_params=PARAMS,
        cost_estimate=cost(12 * 10**9, 20 * 10**6),
    )(pre, gate, pre, rows, par, spar)


def scan_bwd(xpre, gate, y, gg, states_in, rows, tok, bc, par, first, heads):
    inner, length = heads * HEAD, gate.shape[1]
    blocks = length // SPAN
    chan_out, row_out, _, _, whole = specs(length)
    chan, row, parb, states, _ = specs(length, first)
    sds = jax.ShapeDtypeStruct
    return pl.pallas_call(
        bwd_kernel,
        grid=(heads,),
        in_specs=[
            chan, chan, chan, chan, states, row,
            whole(2, length), whole(2 * STATE, length), parb,
        ],
        out_specs=[
            chan_out, chan_out, pl.BlockSpec((HEAD, 128), lambda h: (h, 0)), row_out,
            whole(2 * STATE, length),
        ],
        out_shape=[
            sds((inner, length), BF16),
            sds((inner, length), BF16),
            sds((inner, 128), F32),
            sds((heads, 2, length), F32),
            sds((2 * STATE, length), F32),
        ],
        scratch_shapes=[
            pltpu.VMEM((blocks, SPAN, SPAN), F32),
            pltpu.VMEM((blocks, SPAN, SPAN), F32),
            pltpu.VMEM((2 * STATE, length), F32),
        ],
        compiler_params=PARAMS,
        cost_estimate=cost(heads * 3 * 10**9, heads * 2 * 10**6),
    )(xpre, gate, y, gg, states_in, rows, tok, bc, par)


def state_bwd(spre, dbc, spar):
    sds = jax.ShapeDtypeStruct
    return pl.pallas_call(
        state_kernel,
        out_shape=[sds(spre.shape, BF16), sds((spre.shape[0], 128), F32)],
        compiler_params=pltpu.CompilerParams(vmem_limit_bytes=VMEM_LIMIT),
        cost_estimate=cost(10**9, 2 * 10**6),
    )(spre, dbc, spar)


def bits_of(n):
    return n.bit_length() - 1


def swap(v, axis, n, bit):
    return lax.ppermute(v, axis, [(i, i ^ (1 << bit)) for i in range(n)])


def sum_all(v, axis, n):
    for bit in range(bits_of(n)):
        v = v + swap(v, axis, n, bit)
    return v


def gather(v, axis, n, order):
    me = lax.axis_index(axis)
    held = []
    rest = v.shape
    for bit in order:
        got = swap(v, axis, n, bit)
        low = ((me >> bit) & 1) == 0
        dim = sum(1 for b in held if b > bit)
        v = jnp.stack([jnp.where(low, v, got), jnp.where(low, got, v)], axis=dim)
        held.append(bit)
    return v.reshape((n * rest[0],) + rest[1:])


class Halving:
    def __init__(self, v, axis, n, order):
        self.axis, self.n, self.order = axis, n, list(order)
        self.left = list(range(bits_of(n)))[::-1]
        self.v = v.reshape((2,) * len(self.left) + (v.shape[0] // n,) + v.shape[1:])

    def ready(self):
        bit = self.order[0]
        dim = self.left.index(bit)
        mine = (lax.axis_index(self.axis) >> bit) & 1
        self.keep = lax.dynamic_index_in_dim(self.v, mine, dim, keepdims=False)
        self.send = lax.dynamic_index_in_dim(self.v, 1 - mine, dim, keepdims=False)

    def go(self):
        bit = self.order.pop(0)
        self.left.remove(bit)
        got = swap(self.send, self.axis, self.n, bit)
        self.v = self.keep.astype(F32) + got.astype(F32)
        if self.order:
            self.v = self.v.astype(BF16)

    def finish(self):
        while self.order:
            self.ready()
            self.go()
        return self.v


def sum_scatter(v, axis, n, order):
    return Halving(v, axis, n, order).finish()


def step_beside(chains, tok):
    live = [c for c in chains if c.order]
    for c in live:
        c.ready()
    held = lax.optimization_barrier((tok, [c.send for c in live]))
    for c, send in zip(live, held[1]):
        c.send = send
        c.go()
    return held[0]


def local(
    dp_size,
    tp_size,
    stream,
    norm_gain,
    proj_gate,
    proj_input,
    proj_state,
    proj_step,
    conv_input,
    conv_state,
    bias_input,
    bias_state,
    step_bias,
    decay_log,
    skip_gain,
    gate_gain,
    proj_output,
    cotangent,
):
    inner = conv_input.shape[1]
    heads = inner // HEAD
    own_rows = stream.shape[1]
    length = own_rows * tp_size
    blocks = length // SPAN
    dp_order = [0, 1] + list(range(bits_of(dp_size)))[2:][::-1]
    tp_order = list(range(bits_of(tp_size)))[::-1]
    stream_f = stream[0].astype(F32)
    inv_rms = lax.rsqrt(jnp.mean(stream_f * stream_f, axis=-1, keepdims=True) + EPS)
    normed = stream_f * inv_rms
    own_hidden = (normed * norm_gain).astype(BF16)
    dp_gather = list(range(bits_of(dp_size)))[::-1]
    n_state = proj_state.shape[1]
    near_w = gather(
        jnp.concatenate([proj_input, proj_state, proj_step], axis=1), "dp", dp_size, dp_gather
    )
    hidden = gather(own_hidden, "tensor", tp_size, tp_order)
    gate_w = gather(proj_gate, "dp", dp_size, dp_gather)
    out_w = gather(proj_output.T, "dp", dp_size, dp_gather)
    cot = gather(cotangent[0], "tensor", tp_size, tp_order)

    def project(w):
        return jnp.einsum("lp,pr->rl", hidden, w, preferred_element_type=F32)

    pre = project(near_w)
    state_pre, step_pre = pre[inner : inner + n_state], pre[inner + n_state :]
    gate_pre = project(gate_w)

    step_in = step_pre + step_bias[:, None]
    dt = jax.nn.softplus(step_in)
    neg = -jnp.exp(decay_log)[:, None]
    rate = neg * dt
    tri = jnp.triu(jnp.ones((SPAN, SPAN), F32))
    cum = jnp.einsum(
        "hbt,tq->hbq", rate.reshape(heads, blocks, SPAN), tri, precision=lax.Precision.HIGHEST
    ).reshape(heads, length)
    rows = jnp.stack([cum, dt], axis=1)
    zero = jnp.zeros((inner, 1), F32)
    par = jnp.concatenate(
        [
            conv_input.T,
            bias_input[:, None],
            jnp.repeat(skip_gain, HEAD)[:, None],
            gate_gain[:, None],
            zero,
        ],
        axis=1,
    )
    spar = jnp.concatenate(
        [conv_state.T, bias_state[:, None], jnp.zeros((n_state, 3), F32)], axis=1
    )
    y, mixed, square, states, bc = scan_fwd(pre, gate_pre, rows, par, spar)

    grad_gated = jnp.einsum("le,ec->cl", cot, out_w, preferred_element_type=F32)
    inner_dot = jnp.sum(grad_gated * gate_gain[:, None] * mixed, axis=0, keepdims=True)
    sums = sum_all(jnp.concatenate([square, inner_dot], axis=0), "tensor", tp_size)
    scale = lax.rsqrt(sums[0:1] / DI + EPS)
    tok = jnp.concatenate([scale, scale * scale * scale * (sums[1:2] / DI)], axis=0)
    gated = (mixed * scale * gate_gain[:, None]).astype(BF16)
    grad_out_w = jnp.einsum("cl,le->ec", gated, cot, preferred_element_type=F32).astype(BF16)
    partial_out = jnp.einsum("cl,ec->le", gated, out_w, preferred_element_type=F32).astype(BF16)
    branch = sum_scatter(partial_out, "tensor", tp_size, tp_order)
    output = (stream_f + branch).astype(BF16)

    def weight_grad(g):
        return jnp.einsum("lk,cl->kc", hidden, g, preferred_element_type=F32).astype(BF16)

    out_chain = Halving(grad_out_w, "dp", dp_size, dp_order)
    chains = [out_chain]
    parts = []
    splits = min(4, heads)
    per = heads // splits
    for k in range(splits):
        tok = step_beside(chains, tok)
        part = scan_bwd(
            pre, gate_pre, y, grad_gated, states, rows, tok, bc, par, k * per, per
        )
        parts.append(part)
        both = jnp.concatenate([weight_grad(part[0]), weight_grad(part[1])], axis=1)
        chains.append(Halving(both, "dp", dp_size, dp_order))
    gx, ggate, cols, drows = [jnp.concatenate([p[i] for p in parts], axis=0) for i in range(4)]
    dbc = sum(p[4] for p in parts)
    dbc_total = sum_all(dbc.astype(BF16), "tensor", tp_size)
    gstate, scols = state_bwd(state_pre, dbc_total, spar)
    drate = jnp.einsum(
        "hbt,qt->hbq",
        drows[:, 0].reshape(heads, blocks, SPAN),
        tri,
        precision=lax.Precision.HIGHEST,
    ).reshape(heads, length)
    ddt = drows[:, 1] + drate * neg
    ddecay = jnp.sum(drate * rate, axis=1)
    dstep = ddt * jax.nn.sigmoid(step_in)
    dstep_bias = jnp.sum(dstep, axis=1)
    gstep = dstep.astype(BF16)

    shard_small = sum_scatter(
        weight_grad(jnp.concatenate([gstate, gstep], axis=0)), "dp", dp_size, dp_order
    )
    shard_out = out_chain.finish()
    both = [c.finish() for c in chains[1:]]
    width = per * HEAD
    shard_input = jnp.concatenate([b[:, :width] for b in both], axis=1)
    shard_gate = jnp.concatenate([b[:, width:] for b in both], axis=1)

    def back(g, w):
        return jnp.einsum("cl,nc->ln", g, w, preferred_element_type=F32)

    input_w, state_w = near_w[:, :inner], near_w[:, inner : inner + n_state]
    step_w = near_w[:, inner + n_state :]
    back_terms = back(ggate, gate_w) + back(gx, input_w) + back(gstep, step_w)
    grad_hidden = sum_scatter(back_terms.astype(BF16), "tensor", tp_size, tp_order)
    row_start = lax.axis_index("tensor") * own_rows
    own_gstate = lax.dynamic_slice_in_dim(gstate, row_start, own_rows, 1)
    grad_hidden = grad_hidden + back(own_gstate, state_w)
    weighted_h = grad_hidden * norm_gain
    norm_dot = jnp.mean(weighted_h * normed, axis=-1, keepdims=True)
    grad_stream = (
        cotangent[0].astype(F32) + inv_rms * (weighted_h - normed * norm_dot)
    ).astype(BF16)
    norm_part = sum_all(jnp.sum(grad_hidden * normed, axis=0), "tensor", tp_size)

    pieces = [
        cols[:, :4].T,
        cols[:, 4],
        jnp.sum(cols[:, 5].reshape(heads, HEAD), axis=1),
        cols[:, 6],
        scols[:, :4].T,
        scols[:, 4],
        dstep_bias,
        ddecay,
        norm_part,
    ]
    flat = jnp.concatenate([p.reshape(-1) for p in pieces])
    pad = -flat.shape[0] % 1024
    flat = jnp.pad(flat, (0, pad)).reshape(-1, 128)
    flat = sum_all(flat, "dp", dp_size).reshape(-1)
    done, at = [], 0
    for p in pieces:
        done.append(flat[at : at + p.size].reshape(p.shape))
        at += p.size
    conv_in_g, bias_in_g, skip_g, gain_g, conv_st_g, bias_st_g, step_b_g, decay_g, norm_g = done
    return (
        output[None],
        grad_stream[None],
        norm_g,
        shard_gate,
        shard_input,
        shard_small[:, :n_state],
        shard_small[:, n_state:],
        conv_in_g,
        conv_st_g,
        bias_in_g,
        bias_st_g,
        step_b_g,
        decay_g,
        skip_g,
        gain_g,
        shard_out.T,
    )


def solution(mesh):
    placed = (
        P("dp", "tensor", None),
        P(),
        P("dp", "tensor"),
        P("dp", "tensor"),
        P("dp", None),
        P("dp", "tensor"),
        P(None, "tensor"),
        P(),
        P("tensor"),
        P(),
        P("tensor"),
        P("tensor"),
        P("tensor"),
        P("tensor"),
        P("tensor", "dp"),
        P("dp", "tensor", None),
    )
    dp_size, tp_size = mesh.shape["dp"], mesh.shape["tensor"]

    def run(*args):
        return local(dp_size, tp_size, *args)

    return jax.shard_map(
        run,
        mesh=mesh,
        in_specs=placed,
        out_specs=(
            P("dp", "tensor", None),
            P("dp", "tensor", None),
            P(),
            P("dp", "tensor"),
            P("dp", "tensor"),
            P("dp", None),
            P("dp", "tensor"),
            P(None, "tensor"),
            P(),
            P("tensor"),
            P(),
            P("tensor"),
            P("tensor"),
            P("tensor"),
            P("tensor"),
            P("tensor", "dp"),
        ),
        check_vma=False,
    )
```
